512 devices in a mesh: blk: 16 (over x_hi, y, core), dom: 32 (over z, x_lo).
Axes of the slice: x: 4 (x_hi: 2, x_lo: 2; x = x_hi * 2 + x_lo), y: 4, z: 16, core: 2. Of those that a mesh axis runs over, the one named last changes fastest.
Arguments:
- features: bfloat16 [32, 8192, 256], P('dom', 'blk'), may hold values from -6 to 6
- weight: bfloat16 [256, 256], replicated, may hold values from -0.375 to 0.375
- tiles: bfloat16 [32, 16, 16, 6, 128, 128], P('dom', 'blk'), may hold values from -0.15234375 to 0.15234375
- tile_pos: int32 [32, 16, 16, 6], P('dom', 'blk'), may hold values from 0 to 15, as said below
- tile_count: int32 [32, 16, 16], P('dom', 'blk'), may hold values from 1 to 6
- send_list: int32 [32, 16, 32, 32], P('dom', 'blk'), may hold values from 0 to 511
- send_count: int32 [32, 16, 32], P('dom', 'blk'), may hold values from 0 to 32, as said below
- owner_map: int32 [32, 16, 32, 32], P('dom', 'blk'), may hold values from 0 to 511
- halo_weight: float32 [32, 16, 32, 32], P('dom', 'blk'), may hold values from 0.25 to 1
- cotangent: bfloat16 [32, 8192, 256], P('dom', 'blk'), may hold values from -6 to 6
Outputs:
- layer_out: bfloat16 [32, 8192, 256], P('dom', 'blk')
- feature_grad: bfloat16 [32, 8192, 256], P('dom', 'blk')
- weight_grad: float32 [256, 256], replicated
The draws below stay inside these ranges and needn't reach their ends.
Inputs may be any that keep to these rules, and one draw needn't show every extreme that they name: `tile_pos`: the 6 positions of one row group in one column group are distinct. `send_count`: zero where the peer is the sender's own partition.
All inputs are finite; a program needn't handle non-finite values.
Results may differ from the reference program's by a relative error of at most 0.019.
Values may be sent and summed in bfloat16 or wider, within the bound.
A program may use at most 128 MiB of HBM per device.

```python
import math
import jax
import jax.numpy as jnp
from jax import lax

F = 256
TILE = 128
ROWS = 512
SLOTS = 32
TPG = 6
VERTS = 8192
N_BLK = 16
N_DOM = 32


def draw_tile_pos(key, part):
    count = (ROWS // TILE) ** 2
    scores = jax.random.randint(key, (N_DOM, N_BLK, N_BLK, count), 0, 2 ** 20) * count
    scores = scores + jnp.arange(count, dtype=jnp.int32)
    order = jnp.argsort(scores, axis=-1, stable=True).astype(jnp.int32)
    return order[..., :TPG]


def draw_tile_count(key, part):
    key_level, key_raw, key_spot = jax.random.split(key, 3)
    lowest = (TPG + 1) // 2
    level = jax.random.randint(key_level, (N_DOM, N_BLK, 1), lowest, TPG + 1)
    raw = jax.random.randint(key_raw, (N_DOM, N_BLK, N_BLK), 0, 2 ** 20)
    counts = raw % level + 1
    spot = jax.random.randint(key_spot, (), 0, N_DOM * N_BLK * N_BLK)
    flat = jnp.arange(N_DOM * N_BLK * N_BLK, dtype=jnp.int32).reshape(N_DOM, N_BLK, N_BLK)
    return jnp.where(flat == spot, TPG, counts).astype(jnp.int32)


def draw_send_count(key, part):
    key_raw, key_src, key_grp, key_gap = jax.random.split(key, 4)
    counts = jax.random.randint(key_raw, (N_DOM, N_BLK, N_DOM), 0, SLOTS + 1)
    source = jax.random.randint(key_src, (), 0, N_DOM)
    group = jax.random.randint(key_grp, (), 0, N_BLK)
    target = (source + jax.random.randint(key_gap, (), 1, N_DOM)) % N_DOM
    src_ids = jnp.arange(N_DOM, dtype=jnp.int32)[:, None, None]
    grp_ids = jnp.arange(N_BLK, dtype=jnp.int32)[None, :, None]
    dst_ids = jnp.arange(N_DOM, dtype=jnp.int32)[None, None, :]
    chosen = (src_ids == source) & (grp_ids == group) & (dst_ids == target)
    counts = jnp.where(chosen, SLOTS, counts)
    counts = jnp.where(src_ids == dst_ids, 0, counts)
    return counts.astype(jnp.int32)


def with_ends(array, rng, least, top_value):
    index_at = [jax.random.randint(jax.random.fold_in(rng, axis), (), 0, length) for axis, length in enumerate(array.shape)]
    longest = array.shape.index(max(array.shape))
    beside = index_at[:longest] + [(index_at[longest] + 1) % array.shape[longest]] + index_at[longest + 1:]
    return array.at[tuple(index_at)].set(least).at[tuple(beside)].set(top_value)


def block_scale(own_key, extent, cuts, least, high):
    loudness = 1.0
    for axis_at, parts in cuts:
        heights = jax.random.uniform(jax.random.fold_in(jax.random.fold_in(own_key, 6), axis_at), (parts,), jnp.float32, least / len(cuts), high / len(cuts))
        loudness = loudness * jnp.repeat(jnp.exp(heights), extent[axis_at] // parts).reshape((-1,) + (1,) * (len(extent) - 1 - axis_at))
    return loudness


def scatter_about(own_key, shape, scale, bound, cuts=(), held_as=jnp.bfloat16):
    entries = scale * jax.random.normal(own_key, shape, jnp.float32)
    if cuts:
        entries = entries * block_scale(own_key, shape, cuts, -0.22, 0.18)
    return jnp.clip(entries, -bound, bound).astype(held_as)


def setup_inputs(seed: int = 0) -> dict:
    streams_of = jax.random.split(jax.random.key(seed), 11)
    features = scatter_about(streams_of[0], (N_DOM, VERTS, F), 1.0, 6.0, ((0, 32), (1, 16)))
    weight = scatter_about(streams_of[1], (F, F), F ** -0.5, 0.375)
    tiles = scatter_about(streams_of[2], (N_DOM, N_BLK, N_BLK, TPG, TILE, TILE), ((2.0 * ROWS / (TILE * TILE * N_BLK * TPG)) ** 0.5), 0.15234375, ((0, 32), (1, 16)))
    tile_pos = draw_tile_pos(jax.random.fold_in(streams_of[10], 71), 0)
    tile_count = draw_tile_count(jax.random.fold_in(streams_of[10], 71), 0)
    send_list = with_ends(jax.random.randint(streams_of[5], (N_DOM, N_BLK, N_DOM, SLOTS), 0, ROWS), jax.random.fold_in(streams_of[5], 1), 0, ROWS - 1).astype(jnp.int32)
    send_count = draw_send_count(jax.random.fold_in(streams_of[10], 71), 0)
    owner_map = with_ends(jax.random.randint(streams_of[7], (N_DOM, N_BLK, N_DOM, SLOTS), 0, ROWS), jax.random.fold_in(streams_of[7], 1), 0, ROWS - 1).astype(jnp.int32)
    halo_weight = jnp.clip(jnp.exp(math.log(1.0) - 1.3862944 * jax.random.uniform(streams_of[8], (N_DOM, N_BLK, N_DOM, SLOTS), jnp.float32) ** block_scale(streams_of[8], (N_DOM, N_BLK, N_DOM, SLOTS), ((0, 32), (1, 16)), -0.2, 0.2)), 0.25, 1.0)
    cotangent = scatter_about(streams_of[9], (N_DOM, VERTS, F), 1.0, 6.0, ((0, 32), (1, 16)))
    return {"features": features, "weight": weight, "tiles": tiles, "tile_pos": tile_pos, "tile_count": tile_count, "send_list": send_list, "send_count": send_count, "owner_map": owner_map, "halo_weight": halo_weight, "cotangent": cotangent}


def spread_rows(tile_set, positions, counts, panel, per):
    groups, slots = positions.shape
    tile = tile_set.shape[-1]
    width = panel.shape[-1]
    grid = panel.reshape(groups, per, tile, width)
    column = positions % per
    row_tile = positions // per
    picked = grid[jnp.arange(groups)[:, None], column]
    product = jnp.einsum("gtij,gtjf->gtif", tile_set.astype(jnp.float32), picked.astype(jnp.float32))
    live = jnp.arange(slots)[None, :] < counts[:, None]
    select = ((row_tile[..., None] == jnp.arange(per)[None, None, :]) & live[..., None]).astype(jnp.float32)
    return jnp.einsum("gtif,gtr->rif", product, select).reshape(per * tile, width)


def spread_cols(tile_set, positions, counts, grad_rows, per):
    groups, slots = positions.shape
    tile = tile_set.shape[-1]
    width = grad_rows.shape[-1]
    grid = grad_rows.reshape(per, tile, width)
    column = positions % per
    row_tile = positions // per
    picked = grid[row_tile]
    product = jnp.einsum("gtij,gtif->gtjf", tile_set.astype(jnp.float32), picked.astype(jnp.float32))
    live = jnp.arange(slots)[None, :] < counts[:, None]
    select = ((column[..., None] == jnp.arange(per)[None, None, :]) & live[..., None]).astype(jnp.float32)
    return jnp.einsum("gtjf,gtc->gcjf", product, select).reshape(groups * per * tile, width)


def reference(features, weight, tiles, tile_pos, tile_count, send_list, send_count, owner_map, halo_weight, cotangent):
    n_dom, verts, width = features.shape
    n_blk = tiles.shape[1]
    rows = verts // n_blk
    tile = tiles.shape[-1]
    per = rows // tile
    slots = send_list.shape[-1]
    projected = jnp.dot(features.reshape(-1, width), weight, preferred_element_type=jnp.float32)
    projected = projected.astype(jnp.bfloat16).reshape(n_dom, verts, width)

    def forward_one(index):
        part_id = index // n_blk
        group = index % n_blk
        return spread_rows(tiles[part_id, group], tile_pos[part_id, group], tile_count[part_id, group], projected[part_id], per)

    local = lax.map(forward_one, jnp.arange(n_dom * n_blk)).reshape(n_dom, n_blk, rows, width)

    proj_blocks = projected.reshape(n_dom, n_blk, rows, width)
    src_index = jnp.arange(n_dom)[:, None, None, None]
    grp_index = jnp.arange(n_blk)[None, :, None, None]
    live = (jnp.arange(slots)[None, None, None, :] < send_count[..., None])[..., None]
    sent = jnp.where(live, proj_blocks[src_index, grp_index, send_list], jnp.zeros((), jnp.bfloat16))
    received = jnp.transpose(sent, (2, 1, 0, 3, 4))

    def halo_one(target):
        incoming = received[target].astype(jnp.float32) * halo_weight[target][..., None]
        flat_owner = (jnp.arange(n_blk)[:, None, None] * rows + owner_map[target]).reshape(-1)
        summed = jax.ops.segment_sum(incoming.reshape(-1, width), flat_owner, num_segments=n_blk * rows)
        return summed.reshape(n_blk, rows, width)

    halo_sum = lax.map(halo_one, jnp.arange(n_dom))
    aggregated = local + halo_sum
    layer_out = aggregated.astype(jnp.bfloat16).reshape(n_dom, verts, width)

    grad_blocks = cotangent.reshape(n_dom, n_blk, rows, width)
    back = halo_weight[..., None] * grad_blocks[src_index, grp_index, owner_map].astype(jnp.float32)
    back = back.astype(jnp.bfloat16)
    returned = jnp.transpose(back, (2, 1, 0, 3, 4))
    returned = jnp.where(live, returned, jnp.zeros((), jnp.bfloat16))

    def back_one(source):
        flat_rows = (jnp.arange(n_blk)[:, None, None] * rows + send_list[source]).reshape(-1)
        summed = jax.ops.segment_sum(returned[source].astype(jnp.float32).reshape(-1, width), flat_rows, num_segments=n_blk * rows)
        return summed

    halo_back = lax.map(back_one, jnp.arange(n_dom))

    def grad_part(part_id):
        def step(carry, group):
            grad_rows = lax.dynamic_slice_in_dim(cotangent[part_id], group * rows, rows, 0)
            partial_value = spread_cols(tiles[part_id, group], tile_pos[part_id, group], tile_count[part_id, group], grad_rows, per)
            rounded = lax.optimization_barrier(partial_value.astype(jnp.bfloat16))
            return carry + rounded.astype(jnp.float32), None

        start = jnp.zeros((verts, width), jnp.float32)
        total, unused = lax.scan(step, start, jnp.arange(n_blk))
        return total

    local_grad = lax.map(grad_part, jnp.arange(n_dom))
    proj_grad = (local_grad + halo_back).astype(jnp.bfloat16)
    flat_grad = proj_grad.reshape(-1, width)
    feature_grad = jnp.dot(flat_grad, weight.T, preferred_element_type=jnp.float32).astype(jnp.bfloat16)
    feature_grad = feature_grad.reshape(n_dom, verts, width)
    weight_grad = jnp.dot(features.reshape(-1, width).T, flat_grad, preferred_element_type=jnp.float32)
    weight_grad = weight_grad * (float(n_dom * verts) ** -0.5)
    return layer_out, feature_grad, weight_grad
```

```python
import functools

import jax
import jax.numpy as jnp
from jax import lax
from jax.experimental import pallas as pl
from jax.experimental.pallas import tpu as pltpu
from jax.sharding import PartitionSpec as P

MESH = pl.DeviceIdType.MESH
NB = 16
ND = 32
CHIPS = NB // 2
TILE = 128
PER = 4
ROWS = TILE * PER
TPG = 6
F = 256
SLOTS = 32
LIST = ND * SLOTS
PIECE = F // NB
NEAR = 8
FAR = ND // NEAR
MIB = 1 << 20

bf16 = jnp.bfloat16
f32 = jnp.float32


def dot(a, b, ca=1, cb=0):
    return lax.dot_general(a, b, (((ca,), (cb,)), ((), ())), preferred_element_type=f32)


def local_kernel(
    pos_ref,
    count_ref,
    tiles_ref,
    feats_ref,
    weight_ref,
    cot_ref,
    send_ref,
    owner_ref,
    hw_ref,
    adj_ref,
    partial_ref,
    proj_ref,
    out_ref,
    back_ref,
    pick_ref,
    high_ref,
    low_ref,
):
    c = pl.program_id(0)

    @pl.when(c == 0)
    def _():
        projected = dot(feats_ref[...], weight_ref[...]).astype(bf16)
        proj_ref[...] = projected

        def build(i, carry):
            at = pl.ds(pl.multiple_of(i * TILE, TILE), TILE)
            row = lax.broadcasted_iota(jnp.int32, (TILE, LIST), 0) + i * TILE
            pick_ref[at, :] = jnp.where(row == send_ref[...], 1.0, 0.0).astype(bf16)
            hw = hw_ref[...]
            high = hw.astype(bf16).astype(f32)
            mine = row == owner_ref[...]
            high_ref[at, :] = jnp.where(mine, high, 0.0).astype(bf16)
            low_ref[at, :] = jnp.where(mine, hw - high, 0.0).astype(bf16)
            return carry

        lax.fori_loop(0, PER, build, 0)
        out_ref[...] = dot(pick_ref[...], projected, 0, 0).astype(bf16)
        cot = cot_ref[...]
        back = dot(high_ref[...], cot, 0, 0) + dot(low_ref[...], cot, 0, 0)
        back_ref[...] = back.astype(bf16)

    adj_ref[...] = jnp.zeros_like(adj_ref)
    for t in range(TPG):

        @pl.when(t < count_ref[c])
        def _():
            pos = pos_ref[c * TPG + t]
            r = pl.multiple_of(pos // PER * TILE, TILE)
            k = pl.multiple_of(pos % PER * TILE, TILE)
            adj_ref[0, pl.ds(r, TILE), pl.ds(k, TILE)] = tiles_ref[0, t]

    partial_ref[0, 0] = dot(adj_ref[0], cot_ref[...], 0, 0).astype(bf16)


def local_part(pos, count, tiles, feats, weight, cot, send, owner, hw):
    whole = lambda *shape: pl.BlockSpec(shape, lambda c, *_: (0,) * len(shape))
    shape = jax.ShapeDtypeStruct
    return pl.pallas_call(
        local_kernel,
        grid_spec=pltpu.PrefetchScalarGridSpec(
            num_scalar_prefetch=2,
            grid=(NB,),
            in_specs=[
                pl.BlockSpec((1, TPG, TILE, TILE), lambda c, *_: (c, 0, 0, 0)),
                whole(ROWS, F),
                whole(F, F),
                whole(ROWS, F),
                whole(1, LIST),
                whole(1, LIST),
                whole(1, LIST),
            ],
            out_specs=[
                pl.BlockSpec((1, ROWS, ROWS), lambda c, *_: (c, 0, 0)),
                pl.BlockSpec((1, 1, ROWS, F), lambda c, *_: (c % 2, c // 2, 0, 0)),
                whole(ROWS, F),
                whole(LIST, F),
                whole(LIST, F),
                whole(ROWS, LIST),
                whole(ROWS, LIST),
                whole(ROWS, LIST),
            ],
        ),
        out_shape=[
            shape((NB, ROWS, ROWS), bf16),
            shape((2, CHIPS, ROWS, F), bf16),
            shape((ROWS, F), bf16),
            shape((LIST, F), bf16),
            shape((LIST, F), bf16),
            shape((ROWS, LIST), bf16),
            shape((ROWS, LIST), bf16),
            shape((ROWS, LIST), bf16),
        ],
        compiler_params=pltpu.CompilerParams(vmem_limit_bytes=40 * MIB),
    )(pos, count, tiles, feats, weight, cot, send, owner, hw)


def mesh_kernel(
    adj_hbm,
    partial_hbm,
    out_hbm,
    back_hbm,
    pick_hbm,
    high_hbm,
    low_hbm,
    proj_ref,
    feats_ref,
    weight_ref,
    layer_ref,
    fgrad_ref,
    wgrad_ref,
    adj,
    own,
    pick,
    high,
    low,
    pair_got,
    pair_sum,
    rs_got,
    returned,
    incoming,
    gathered,
    acc,
    term,
    chunk_a,
    chunk_b,
    chunk_c,
    got_a,
    got_b,
    got_c,
    total,
    load_sem,
    pair_send,
    pair_recv,
    rs_send,
    rs_recv,
    back_send,
    back_recv,
    out_send,
    out_recv,
    ag_send,
    ag_recv,
    sib_send,
    sib_recv,
    ar_send,
    ar_recv,
):
    b = lax.axis_index("blk")
    d = lax.axis_index("dom")
    core = lax.rem(b, 2)
    chip = b // 2
    sibling = b + 1 - 2 * core

    def remote(src, dst, send, recv, blk, dom):
        return pltpu.make_async_remote_copy(
            src_ref=src,
            dst_ref=dst,
            send_sem=send,
            recv_sem=recv,
            device_id=(blk, dom),
            device_id_type=MESH,
        )

    def await_bytes(ref, sem):
        pltpu.make_async_copy(ref, ref, sem).wait()

    def loop(lo, hi, body):
        def step(i, carry):
            body(i)
            return carry

        lax.fori_loop(lo, hi, step, 0)

    def block(i, n):
        return pl.ds(pl.multiple_of(i * n, n), n)

    loads = [
        pltpu.make_async_copy(src, dst, load_sem.at[i])
        for i, (src, dst) in enumerate(
            (
                (partial_hbm.at[core], own),
                (pick_hbm, pick),
                (adj_hbm, adj),
                (high_hbm, high),
                (low_hbm, low),
            )
        )
    ]
    for load in loads:
        load.start()

    barrier = pltpu.get_barrier_semaphore()

    def greet_dom(k):
        pl.semaphore_signal(
            barrier, inc=1, device_id=(b, lax.rem(d + k, ND)), device_id_type=MESH
        )

    def greet_blk(k):
        pl.semaphore_signal(
            barrier, inc=1, device_id=(lax.rem(b + k, NB), d), device_id_type=MESH
        )

    loop(1, ND, greet_dom)
    loop(1, NB, greet_blk)
    pl.semaphore_wait(barrier, ND + NB - 2)

    def pair_copy(j):
        at = lax.rem(chip + j, CHIPS)
        return remote(
            partial_hbm.at[1 - core, at],
            pair_got.at[at],
            pair_send,
            pair_recv.at[j],
            sibling,
            d,
        )

    loop(1, CHIPS + 1, lambda j: pair_copy(j).start())

    def dom_send(src, dst, send, recv):
        def body(i):
            half = i // 2
            k = half + 1 + lax.rem(i, 2) * (ND - 2 - 2 * half)
            q = lax.rem(d + k, ND)
            remote(
                src.at[block(q, SLOTS)], dst.at[block(d, SLOTS)], send, recv, b, q
            ).start()

        loop(0, ND - 1, body)

    dom_send(back_hbm, returned, back_send, back_recv)

    loads[0].wait()

    def rs_copy(j):
        at = lax.rem(chip + j, CHIPS)
        return remote(
            pair_sum.at[j], rs_got.at[j], rs_send, rs_recv.at[j], 2 * at + core, d
        )

    def pair_step(j):
        at = lax.rem(chip + j, CHIPS)
        pair_copy(j).wait_recv()
        both = own[at].astype(f32) + pair_got[at].astype(f32)
        pair_sum[j] = both.astype(bf16)
        rs_copy(j).start()

    loop(1, CHIPS, pair_step)

    def ag_copy(j):
        to = 2 * lax.rem(chip + j, CHIPS) + core
        return remote(proj_ref, gathered.at[b], ag_send, ag_recv.at[j], to, d)

    def sib_copy(j):
        at = 2 * lax.rem(chip + CHIPS - j, CHIPS) + core
        return remote(
            gathered.at[at], gathered.at[at], sib_send, sib_recv.at[j], sibling, d
        )

    loop(1, CHIPS, lambda j: ag_copy(j).start())
    remote(proj_ref, gathered.at[b], sib_send, sib_recv.at[0], sibling, d).start()
    dom_send(out_hbm, incoming, out_send, out_recv)

    pair_copy(CHIPS).wait_recv()
    acc[...] = own[chip].astype(f32) + pair_got[chip].astype(f32)
    zero = jnp.zeros((SLOTS, F), bf16)
    returned[block(d, SLOTS), :] = zero
    incoming[block(d, SLOTS), :] = zero

    def rs_step(j):
        rs_copy(j).wait_recv()
        acc[...] += rs_got[j].astype(f32)

    loop(1, CHIPS, rs_step)
    others = pl.ds(0, LIST - SLOTS)
    await_bytes(returned.at[others], back_recv)
    loads[1].wait()
    grad = (acc[...] + dot(pick[...], returned[...])).astype(bf16)
    term[...] = dot(feats_ref[...], grad, 0, 0)

    def blk_send(src_of, dst_of, stage):
        def body(k):
            to = lax.rem(b + k, NB)
            remote(
                src_of(to), dst_of(k), ar_send.at[stage], ar_recv.at[stage], to, d
            ).start()

        loop(1, NB, body)

    blk_send(lambda to: term.at[block(to, PIECE)], lambda k: got_a.at[k], 0)
    fgrad_ref[...] = dot(grad, weight_ref[...], 1, 1).astype(bf16)
    loads[2].wait()

    acc[...] = dot(adj[b], proj_ref[...])

    def ag_step(j):
        at = 2 * lax.rem(chip + CHIPS - j, CHIPS) + core
        ag_copy(j).wait_recv()
        sib_copy(j).start()
        acc[...] += dot(adj[at], gathered[at])

    loop(1, CHIPS, ag_step)

    def sib_step(j):
        at = 2 * lax.rem(chip + CHIPS - j, CHIPS) + 1 - core
        sib_copy(j).wait_recv()
        acc[...] += dot(adj[at], gathered[at])

    await_bytes(got_a.at[pl.ds(1, NB - 1)], ar_recv.at[0])
    piece = term[block(b, PIECE), :]
    for k in range(1, NB):
        piece = piece + got_a[k]
    chunk_a[...] = piece

    def near_send(k):
        to = d // NEAR * NEAR + lax.rem(lax.rem(d, NEAR) + k, NEAR)
        remote(chunk_a, got_b.at[k], ar_send.at[1], ar_recv.at[1], b, to).start()

    loop(1, NEAR, near_send)
    loop(0, 4, sib_step)
    await_bytes(got_b.at[pl.ds(1, NEAR - 1)], ar_recv.at[1])
    piece = chunk_a[...]
    for k in range(1, NEAR):
        piece = piece + got_b[k]
    chunk_b[...] = piece

    def far_send(k):
        to = lax.rem(d + k * NEAR, ND)
        remote(chunk_b, got_c.at[k], ar_send.at[2], ar_recv.at[2], b, to).start()

    loop(1, FAR, far_send)
    loop(4, CHIPS, sib_step)
    await_bytes(got_c.at[pl.ds(1, FAR - 1)], ar_recv.at[2])
    piece = chunk_b[...]
    for k in range(1, FAR):
        piece = piece + got_c[k]
    piece = piece * (float(NB * ND * ROWS) ** -0.5)
    chunk_c[...] = piece
    blk_send(lambda to: chunk_c, lambda k: total.at[block(b, PIECE)], 3)
    total[block(b, PIECE), :] = piece

    loads[3].wait()
    loads[4].wait()
    await_bytes(incoming.at[others], out_recv)
    came = incoming[...]
    halo = dot(high[...], came) + dot(low[...], came)
    layer_ref[...] = (acc[...] + halo).astype(bf16)
    await_bytes(total.at[pl.ds(0, F - PIECE)], ar_recv.at[3])
    wgrad_ref[...] = total[...]

    await_bytes(pair_got, pair_send)
    await_bytes(rs_got.at[pl.ds(1, CHIPS - 1)], rs_send)
    await_bytes(returned.at[others], back_send)
    await_bytes(incoming.at[others], out_send)
    await_bytes(rs_got.at[pl.ds(1, CHIPS - 1)], ag_send)
    await_bytes(rs_got, sib_send)
    await_bytes(got_a.at[pl.ds(1, NB - 1)], ar_send.at[0])
    await_bytes(got_b.at[pl.ds(1, NEAR - 1)], ar_send.at[1])
    await_bytes(got_c.at[pl.ds(1, FAR - 1)], ar_send.at[2])
    await_bytes(got_a.at[pl.ds(1, NB - 1)], ar_send.at[3])


def mesh_part(adj, partial, out, back, pick, high, low, proj, feats, weight):
    shape = jax.ShapeDtypeStruct
    far = pl.BlockSpec(memory_space=pl.ANY)
    near = pl.BlockSpec(memory_space=pltpu.VMEM)
    dma = pltpu.SemaphoreType.DMA
    vmem = pltpu.VMEM
    return pl.pallas_call(
        mesh_kernel,
        out_shape=[
            shape((ROWS, F), bf16),
            shape((ROWS, F), bf16),
            shape((F, F), f32),
        ],
        in_specs=[far] * 7 + [near] * 3,
        out_specs=[near] * 3,
        scratch_shapes=[
            vmem((NB, ROWS, ROWS), bf16),
            vmem((CHIPS, ROWS, F), bf16),
            vmem((ROWS, LIST), bf16),
            vmem((ROWS, LIST), bf16),
            vmem((ROWS, LIST), bf16),
            vmem((CHIPS, ROWS, F), bf16),
            vmem((CHIPS, ROWS, F), bf16),
            vmem((CHIPS, ROWS, F), bf16),
            vmem((LIST, F), bf16),
            vmem((LIST, F), bf16),
            vmem((NB, ROWS, F), bf16),
            vmem((ROWS, F), f32),
            vmem((F, F), f32),
            vmem((PIECE, F), f32),
            vmem((PIECE, F), f32),
            vmem((PIECE, F), f32),
            vmem((NB, PIECE, F), f32),
            vmem((NEAR, PIECE, F), f32),
            vmem((FAR, PIECE, F), f32),
            vmem((F, F), f32),
            dma((5,)),
            dma,
            dma((CHIPS + 1,)),
            dma,
            dma((CHIPS,)),
            dma,
            dma,
            dma,
            dma,
            dma,
            dma((CHIPS,)),
            dma,
            dma((CHIPS,)),
            dma((4,)),
            dma((4,)),
        ],
        compiler_params=pltpu.CompilerParams(
            collective_id=0, has_side_effects=True, vmem_limit_bytes=48 * MIB
        ),
    )(adj, partial, out, back, pick, high, low, proj, feats, weight)


def on_device(
    features,
    weight,
    tiles,
    tile_pos,
    tile_count,
    send_list,
    send_count,
    owner_map,
    halo_weight,
    cotangent,
):
    live = jnp.arange(SLOTS)[None, :] < send_count[0, 0][:, None]
    send = jnp.where(live, send_list[0, 0], -1).reshape(1, LIST)
    adj, partial, proj, out, back, pick, high, low = local_part(
        tile_pos.reshape(-1),
        tile_count.reshape(-1),
        tiles[0, 0],
        features[0],
        weight,
        cotangent[0],
        send,
        owner_map.reshape(1, LIST),
        halo_weight.reshape(1, LIST),
    )
    layer_out, feature_grad, weight_grad = mesh_part(
        adj, partial, out, back, pick, high, low, proj, features[0], weight
    )
    return (layer_out[None], feature_grad[None], weight_grad)


def solution(mesh):
    return jax.shard_map(
        on_device,
        mesh=mesh,
        in_specs=(
            P("dom", "blk", None),
            P(),
            P("dom", "blk", None, None, None, None),
            P("dom", "blk", None, None),
            P("dom", "blk", None),
            P("dom", "blk", None, None),
            P("dom", "blk", None),
            P("dom", "blk", None, None),
            P("dom", "blk", None, None),
            P("dom", "blk", None),
        ),
        out_specs=(P("dom", "blk", None), P("dom", "blk", None), P()),
        check_vma=False,
    )
```

```python
import functools

import jax
import jax.numpy as jnp
from jax import lax
from jax.experimental import pallas as pl
from jax.experimental.pallas import tpu as pltpu
from jax.sharding import PartitionSpec as P

MESH = pl.DeviceIdType.MESH
NB = 16
ND = 32
CHIPS = NB // 2
COL = 4
HALF = 256
TILE = 128
PER = 4
ROWS = TILE * PER
TPG = 6
F = 256
SLOTS = 32
LIST = ND * SLOTS
PIECE = F // NB
NEAR = 8
FAR = ND // NEAR
MIB = 1 << 20

bf16 = jnp.bfloat16
f32 = jnp.float32


def dot(a, b, ca=1, cb=0):
    return lax.dot_general(a, b, (((ca,), (cb,)), ((), ())), preferred_element_type=f32)


def mesh_kernel(
    pos_ref,
    count_ref,
    tiles_hbm,
    feats_hbm,
    cot_hbm,
    weight_hbm,
    send_hbm,
    live_hbm,
    owner_hbm,
    hw_hbm,
    layer_ref,
    fgrad_ref,
    wgrad_ref,
    tiles,
    feats,
    cot,
    weight,
    send_rows,
    owner_rows,
    hw_rows,
    live_row,
    adj,
    pick,
    high,
    low,
    outgoing,
    back,
    returned,
    incoming,
    other,
    own,
    pair_got,
    pair_sum,
    rs_y,
    rs_x,
    rs_got,
    gathered,
    acc,
    term,
    term16,
    chunk,
    got_a,
    got_b,
    got_c,
    total,
    load_sem,
    pair_send,
    pair_recv,
    rs_send,
    rs_recv,
    sum_send,
    sum_recv,
    back_send,
    back_recv,
    out_send,
    out_recv,
    ag_send,
    ag_recv,
    diag_send,
    diag_recv,
    sib_send,
    sib_recv,
    ar_send,
    ar_recv,
):
    b = lax.axis_index("blk")
    d = lax.axis_index("dom")
    core = lax.rem(b, 2)
    chip = b // 2
    sibling = b + 1 - 2 * core
    column = chip // COL
    y = lax.rem(chip, COL)

    def chip_at(s):
        return lax.rem(column + s // COL, 2) * COL + lax.rem(y + lax.rem(s, COL), COL)

    def device_at(s):
        return 2 * chip_at(s) + core

    def remote(src, dst, send, recv, blk, dom):
        return pltpu.make_async_remote_copy(
            src_ref=src,
            dst_ref=dst,
            send_sem=send,
            recv_sem=recv,
            device_id=(blk, dom),
            device_id_type=MESH,
        )

    def await_bytes(ref, sem):
        pltpu.make_async_copy(ref, ref, sem).wait()

    def loop(lo, hi, body):
        def step(i, carry):
            body(i)
            return carry

        lax.fori_loop(lo, hi, step, 0)

    def block(i, n):
        return pl.ds(pl.multiple_of(i * n, n), n)

    loads = [
        pltpu.make_async_copy(src, dst, load_sem.at[i])
        for i, (src, dst) in enumerate(
            (
                (send_hbm, send_rows),
                (owner_hbm, owner_rows),
                (hw_hbm, hw_rows),
                (live_hbm, live_row),
                (feats_hbm, feats),
                (cot_hbm, cot),
                (tiles_hbm, tiles.at[:, pl.ds(1, TPG)]),
                (weight_hbm, weight),
            )
        )
    ]
    for load in loads:
        load.start()

    barrier = pltpu.get_barrier_semaphore()

    def greet_dom(k):
        pl.semaphore_signal(
            barrier, inc=1, device_id=(b, lax.rem(d + k, ND)), device_id_type=MESH
        )

    def greet_blk(k):
        pl.semaphore_signal(
            barrier, inc=1, device_id=(lax.rem(b + k, NB), d), device_id_type=MESH
        )

    loop(1, ND, greet_dom)
    loop(1, NB, greet_blk)

    for load in loads[:5]:
        load.wait()
    hw = hw_rows[...]
    hw_high = hw.astype(bf16)
    hw_low = (hw - hw_high.astype(f32)).astype(bf16)
    send = send_rows[...]
    owner = owner_rows[...]
    as_bf16 = lambda x: x.astype(f32).astype(bf16)
    stack = [as_bf16(send // 16), as_bf16(send % 16)]
    stack += [as_bf16(owner // 16), as_bf16(owner % 16), hw_high, hw_low]
    lane = lax.broadcasted_iota(jnp.int32, (SLOTS, LIST), 1)
    line = lax.broadcasted_iota(jnp.int32, (SLOTS, LIST), 0)
    spread = jnp.where(lane % SLOTS == line, 1.0, 0.0).astype(bf16)
    mine = lane // SLOTS == line

    def flat(x):
        return jnp.sum(jnp.where(mine, dot(x, spread), 0.0), axis=0, keepdims=True)

    rows = [flat(x) for x in stack]
    counts = jnp.broadcast_to(as_bf16(live_row[...]), (8, ND))
    count_row = dot(counts, jnp.where(mine, 1.0, 0.0).astype(bf16))[:1]
    slot = (lax.broadcasted_iota(jnp.int32, (1, LIST), 1) % SLOTS).astype(f32)
    send_row = jnp.where(slot < count_row, rows[0] * 16.0 + rows[1], -1.0)
    owner_row = rows[2] * 16.0 + rows[3]

    for i in range(PER):
        at = pl.ds(i * TILE, TILE)
        row = (lax.broadcasted_iota(jnp.int32, (TILE, LIST), 0) + i * TILE).astype(f32)
        pick[at, :] = jnp.where(row == send_row, 1.0, 0.0).astype(bf16)
    outgoing[...] = dot(pick[...], feats[...], 0, 0).astype(bf16)

    pl.semaphore_wait(barrier, ND + NB - 2)

    def ag_copy(s):
        return remote(
            feats, gathered.at[b], ag_send, ag_recv.at[s], device_at(s), d
        )

    def back_at(s):
        return lax.rem(column + s // COL, 2) * COL + lax.rem(y + COL - lax.rem(s, COL), COL)

    def sib_copy(s):
        at = gathered.at[2 * back_at(s) + core]
        return remote(at, at, sib_send, sib_recv.at[s], sibling, d)

    first, second = pl.ds(0, HALF), pl.ds(HALF, HALF)

    def diag_y(j):
        at = gathered.at[device_at(COL), first]
        return remote(at, at, diag_send, diag_recv.at[j], device_at(j), d)

    def diag_x(j):
        at = gathered.at[2 * back_at(j) + core, second]
        return remote(at, at, diag_send, diag_recv.at[COL + j], device_at(COL), d)

    ag_copy(COL).start()
    loop(1, COL, lambda s: ag_copy(s).start())
    remote(feats, gathered.at[b], sib_send, sib_recv.at[0], sibling, d).start()

    def dom_send(src, dst, send, recv):
        def body(i):
            half = i // 2
            k = half + 1 + lax.rem(i, 2) * (ND - 2 - 2 * half)
            q = lax.rem(d + k, ND)
            remote(
                src.at[block(q, SLOTS)], dst.at[block(d, SLOTS)], send, recv, b, q
            ).start()

        loop(0, ND - 1, body)

    dom_send(outgoing, incoming, out_send, out_recv)

    loads[5].wait()
    for i in range(PER):
        at = pl.ds(i * TILE, TILE)
        row = (lax.broadcasted_iota(jnp.int32, (TILE, LIST), 0) + i * TILE).astype(f32)
        hit = row == owner_row
        high[at, :] = jnp.where(hit, rows[4], 0.0).astype(bf16)
        low[at, :] = jnp.where(hit, rows[5], 0.0).astype(bf16)
    back[...] = (
        dot(high[...], cot[...], 0, 0) + dot(low[...], cot[...], 0, 0)
    ).astype(bf16)
    dom_send(back, returned, back_send, back_recv)

    zero = jnp.zeros((TILE, TILE), bf16)

    def clear(c):
        tiles[c, 0] = zero

    loop(0, NB, clear)
    loads[6].wait()

    def share(c):
        live = count_ref[c]
        spots = [jnp.where(t < live, pos_ref[t, 0, c], -1) for t in range(TPG)]
        for p in range(PER * PER):
            found = 0
            for t in range(TPG):
                found = jnp.where(spots[t] == p, t + 1, found)
            r, k = p // PER, p % PER
            adj[c, pl.ds(r * TILE, TILE), pl.ds(k * TILE, TILE)] = tiles[c, found]
        return dot(adj[c], cot[...], 0, 0).astype(bf16)

    def pair_copy(s):
        return remote(
            other.at[s], pair_got.at[s], pair_send, pair_recv.at[s], sibling, d
        )

    def other_step(i):
        s = lax.rem(i + COL + 1, CHIPS)
        other[s] = share(2 * chip_at(s) + 1 - core)
        pair_copy(s).start()

    loop(0, CHIPS, other_step)

    ag_copy(COL).wait_recv()
    loop(1, COL, lambda j: diag_y(j).start())
    sib_copy(COL).start()

    def column_step(s):
        ag_copy(s).wait_recv()
        diag_x(s).start()
        sib_copy(s).start()

    loop(1, COL, column_step)

    def own_step(i):
        s = lax.rem(i + COL + 1, CHIPS)
        own[s] = share(device_at(s))

    loop(0, CHIPS, own_step)

    def rs_first(j):
        return remote(
            pair_sum.at[COL + j, first], rs_y.at[j], rs_send, rs_recv.at[j], device_at(j), d
        )

    def rs_second(j):
        return remote(
            pair_sum.at[COL + j, second],
            rs_x.at[j],
            rs_send,
            rs_recv.at[COL + j],
            device_at(COL),
            d,
        )

    def sum_copy(s):
        return remote(
            pair_sum.at[s], rs_got.at[s], sum_send, sum_recv.at[s], device_at(s), d
        )

    def pair_step(s):
        pair_copy(s).wait_recv()
        pair_sum[s] = (own[s].astype(f32) + pair_got[s].astype(f32)).astype(bf16)

    def diag_step(j):
        pair_step(COL + j)
        rs_first(j).start()
        rs_second(j).start()

    loop(1, COL, diag_step)
    loop(1, COL + 1, pair_step)

    acc[...] = dot(adj[b], feats[...])

    def gain(at):
        acc[...] += dot(adj[at], gathered[at])

    loop(1, COL + 1, lambda s: gain(2 * back_at(s) + core))
    sib_copy(0).wait_recv()
    gain(sibling)

    def diag_wait(j):
        diag_y(j).wait_recv()
        diag_x(j).wait_recv()
        sib_copy(COL + j).start()
        gain(2 * back_at(COL + j) + core)

    loop(1, COL, diag_wait)

    def sib_step(s):
        sib_copy(s).wait_recv()
        gain(2 * back_at(s) + 1 - core)

    loop(1, CHIPS, sib_step)

    none = jnp.zeros((SLOTS, F), bf16)
    incoming[block(d, SLOTS), :] = none
    returned[block(d, SLOTS), :] = none
    others = pl.ds(0, LIST - SLOTS)
    await_bytes(incoming.at[others], out_recv)
    came = incoming[...]
    gained = (acc[...] + dot(high[...], came) + dot(low[...], came)).astype(bf16)
    whole = dot(gained, cot[...], 0, 0)
    term[...] = whole
    term16[...] = whole.astype(bf16)

    def blk_send(src_of, dst_of, stage):
        def body(k):
            to = lax.rem(b + k, NB)
            remote(
                src_of(to), dst_of(k), ar_send.at[stage], ar_recv.at[stage], to, d
            ).start()

        loop(1, NB, body)

    blk_send(lambda to: term16.at[block(to, PIECE)], lambda k: got_a.at[k], 0)
    loads[7].wait()
    layer_ref[...] = dot(gained, weight[...]).astype(bf16)

    await_bytes(got_a.at[pl.ds(1, NB - 1)], ar_recv.at[0])
    piece = term[block(b, PIECE), :]
    for k in range(1, NB):
        piece = piece + got_a[k].astype(f32)

    mine = lax.rem(d, NEAR)
    got_b[mine] = piece.astype(bf16)

    def near_send(k):
        to = d // NEAR * NEAR + lax.rem(mine + k, NEAR)
        at = got_b.at[mine]
        remote(at, at, ar_send.at[1], ar_recv.at[1], b, to).start()

    loop(1, NEAR, near_send)

    def column_sum(j):
        rs_second(j).wait_recv()
        at = pair_sum[j, HALF:].astype(f32) + rs_x[j].astype(f32)
        pair_sum[j, HALF:] = at.astype(bf16)
        sum_copy(j).start()

    def partner_sum(j):
        rs_first(j).wait_recv()

    loop(1, COL, partner_sum)
    both = pair_sum[COL, :HALF].astype(f32)
    for j in range(1, COL):
        both = both + rs_y[j].astype(f32)
    pair_sum[COL, :HALF] = both.astype(bf16)
    sum_copy(COL).start()
    loop(1, COL, column_sum)

    await_bytes(got_b.at[pl.ds(1, NEAR - 1)], ar_recv.at[1])
    piece = got_b[0].astype(f32)
    for k in range(1, NEAR):
        piece = piece + got_b[k].astype(f32)
    group = d // NEAR
    got_c[group] = piece.astype(bf16)

    def far_send(k):
        to = lax.rem(d + k * NEAR, ND)
        at = got_c.at[group]
        remote(at, at, ar_send.at[2], ar_recv.at[2], b, to).start()

    loop(1, FAR, far_send)
    pair_copy(0).wait_recv()
    acc[...] = own[0].astype(f32) + pair_got[0].astype(f32)
    await_bytes(got_c.at[pl.ds(1, FAR - 1)], ar_recv.at[2])
    piece = got_c[0].astype(f32)
    for k in range(1, FAR):
        piece = piece + got_c[k].astype(f32)
    piece = (piece * (float(NB * ND * ROWS) ** -0.5)).astype(bf16)
    chunk[...] = piece
    blk_send(lambda to: chunk, lambda k: total.at[block(b, PIECE)], 3)
    total[block(b, PIECE), :] = piece
    await_bytes(returned.at[others], back_recv)
    acc[...] += dot(pick[...], returned[...])

    def sum_step(s):
        sum_copy(s).wait_recv()
        acc[...] += rs_got[s].astype(f32)

    loop(1, COL + 1, sum_step)
    fgrad_ref[...] = dot(acc[...].astype(bf16), weight[...], 1, 1).astype(bf16)
    await_bytes(total.at[pl.ds(0, F - PIECE)], ar_recv.at[3])
    wgrad_ref[...] = total[...].astype(f32)

    await_bytes(pair_got, pair_send)
    await_bytes(pair_sum.at[pl.ds(0, COL - 1)], rs_send)
    await_bytes(pair_sum.at[pl.ds(0, COL)], sum_send)
    await_bytes(returned.at[others], back_send)
    await_bytes(incoming.at[others], out_send)
    await_bytes(pair_sum.at[pl.ds(0, COL)], ag_send)
    await_bytes(pair_sum.at[pl.ds(0, COL - 1)], diag_send)
    await_bytes(pair_sum, sib_send)
    await_bytes(got_a.at[pl.ds(1, NB - 1)], ar_send.at[0])
    await_bytes(got_b.at[pl.ds(1, NEAR - 1)], ar_send.at[1])
    await_bytes(got_c.at[pl.ds(1, FAR - 1)], ar_send.at[2])
    await_bytes(got_a.at[pl.ds(1, NB - 1)], ar_send.at[3])


def mesh_part(pos, count, tiles, feats, cot, weight, send, live, owner, hw):
    shape = jax.ShapeDtypeStruct
    far = pl.BlockSpec(memory_space=pltpu.HBM)
    near = pl.BlockSpec(memory_space=pltpu.VMEM)
    scalar = pl.BlockSpec(memory_space=pltpu.SMEM)
    dma = pltpu.SemaphoreType.DMA
    vmem = pltpu.VMEM
    return pl.pallas_call(
        mesh_kernel,
        out_shape=[
            shape((ROWS, F), bf16),
            shape((ROWS, F), bf16),
            shape((F, F), f32),
        ],
        in_specs=[scalar] * 2 + [far] * 8,
        out_specs=[near] * 3,
        scratch_shapes=[
            vmem((NB, TPG + 1, TILE, TILE), bf16),
            vmem((ROWS, F), bf16),
            vmem((ROWS, F), bf16),
            vmem((F, F), bf16),
            vmem((ND, SLOTS), jnp.int32),
            vmem((ND, SLOTS), jnp.int32),
            vmem((ND, SLOTS), f32),
            vmem((1, ND), jnp.int32),
            vmem((NB, ROWS, ROWS), bf16),
            vmem((ROWS, LIST), bf16),
            vmem((ROWS, LIST), bf16),
            vmem((ROWS, LIST), bf16),
            vmem((LIST, F), bf16),
            vmem((LIST, F), bf16),
            vmem((LIST, F), bf16),
            vmem((LIST, F), bf16),
            vmem((CHIPS, ROWS, F), bf16),
            vmem((CHIPS, ROWS, F), bf16),
            vmem((CHIPS, ROWS, F), bf16),
            vmem((CHIPS, ROWS, F), bf16),
            vmem((COL, HALF, F), bf16),
            vmem((COL, HALF, F), bf16),
            vmem((COL + 1, ROWS, F), bf16),
            vmem((NB, ROWS, F), bf16),
            vmem((ROWS, F), f32),
            vmem((F, F), f32),
            vmem((F, F), bf16),
            vmem((PIECE, F), bf16),
            vmem((NB, PIECE, F), bf16),
            vmem((NEAR, PIECE, F), bf16),
            vmem((FAR, PIECE, F), bf16),
            vmem((F, F), bf16),
            dma((8,)),
            dma,
            dma((CHIPS,)),
            dma,
            dma((CHIPS,)),
            dma,
            dma((COL + 1,)),
            dma,
            dma,
            dma,
            dma,
            dma,
            dma((COL + 1,)),
            dma,
            dma((CHIPS,)),
            dma,
            dma((CHIPS,)),
            dma((4,)),
            dma((4,)),
        ],
        compiler_params=pltpu.CompilerParams(
            collective_id=0, has_side_effects=True, vmem_limit_bytes=60 * MIB
        ),
    )(pos, count, tiles, feats, cot, weight, send, live, owner, hw)


def final_kernel(*refs):
    sources, targets, held, (load_sem, store_sem) = (
        refs[:3],
        refs[3:6],
        refs[6:9],
        refs[9:],
    )
    loads = [
        pltpu.make_async_copy(src, at, load_sem.at[i])
        for i, (src, at) in enumerate(zip(sources, held))
    ]
    stores = [
        pltpu.make_async_copy(at, dst, store_sem.at[i])
        for i, (at, dst) in enumerate(zip(held, targets))
    ]
    for load in loads:
        load.start()
    for load, store in zip(loads, stores):
        load.wait()
        store.start()
    for store in stores:
        store.wait()


def final_part(*results):
    far = pl.BlockSpec(memory_space=pltpu.HBM)
    return pl.pallas_call(
        final_kernel,
        out_shape=[jax.ShapeDtypeStruct(x.shape, x.dtype) for x in results],
        in_specs=[far] * 3,
        out_specs=[far] * 3,
        scratch_shapes=[pltpu.VMEM(x.shape, x.dtype) for x in results]
        + [pltpu.SemaphoreType.DMA((3,))] * 2,
        compiler_params=pltpu.CompilerParams(vmem_limit_bytes=60 * MIB),
    )(*results)


def on_device(
    features,
    weight,
    tiles,
    tile_pos,
    tile_count,
    send_list,
    send_count,
    owner_map,
    halo_weight,
    cotangent,
):
    results = mesh_part(
        jnp.transpose(tile_pos, (0, 3, 1, 2))[0],
        tile_count[0, 0],
        tiles[0, 0],
        features[0],
        cotangent[0],
        weight,
        send_list[0, 0],
        send_count[0],
        owner_map[0, 0],
        halo_weight[0, 0],
    )
    layer_out, feature_grad, weight_grad = final_part(*results)
    return (layer_out[None], feature_grad[None], weight_grad)


def solution(mesh):
    return jax.shard_map(
        on_device,
        mesh=mesh,
        in_specs=(
            P("dom", "blk", None),
            P(),
            P("dom", "blk", None, None, None, None),
            P("dom", "blk", None, None),
            P("dom", "blk", None),
            P("dom", "blk", None, None),
            P("dom", "blk", None),
            P("dom", "blk", None, None),
            P("dom", "blk", None, None),
            P("dom", "blk", None),
        ),
        out_specs=(P("dom", "blk", None), P("dom", "blk", None), P()),
        check_vma=False,
    )
```

```python
import functools

import jax
import jax.numpy as jnp
from jax import lax
from jax.experimental import pallas as pl
from jax.experimental.pallas import tpu as pltpu
from jax.sharding import PartitionSpec as P

MESH = pl.DeviceIdType.MESH
NB = 16
ND = 32
CHIPS = NB // 2
COL = 4
HALF = 256
TILE = 128
PER = 4
ROWS = TILE * PER
TPG = 6
F = 256
SLOTS = 32
LIST = ND * SLOTS
PIECE = F // NB
PLANE = 2 * NB
RING = ND // 2
MIB = 1 << 20

bf16 = jnp.bfloat16
f32 = jnp.float32


def dot(a, b, ca=1, cb=0):
    return lax.dot_general(a, b, (((ca,), (cb,)), ((), ())), preferred_element_type=f32)


def mesh_kernel(
    pos_ref,
    count_ref,
    tiles_hbm,
    feats_hbm,
    cot_hbm,
    weight_hbm,
    send_hbm,
    live_hbm,
    owner_hbm,
    hw_hbm,
    layer_ref,
    fgrad_ref,
    wgrad_ref,
    tiles,
    feats,
    cot,
    weight,
    send_rows,
    owner_rows,
    hw_rows,
    live_row,
    adj,
    pick,
    high,
    low,
    outgoing,
    back,
    returned,
    incoming,
    other,
    own,
    pair_got,
    pair_sum,
    rs_y,
    rs_x,
    rs_got,
    gathered,
    acc,
    term,
    term16,
    chunk,
    got_a,
    got_z,
    total,
    load_sem,
    pair_send,
    pair_recv,
    rs_send,
    rs_recv,
    sum_send,
    sum_recv,
    back_send,
    back_recv,
    out_send,
    out_recv,
    ag_send,
    ag_recv,
    rest_recv,
    diag_send,
    diag_recv,
    sib_send,
    sib_recv,
    ar_send,
    ar_recv,
):
    b = lax.axis_index("blk")
    d = lax.axis_index("dom")
    core = lax.rem(b, 2)
    chip = b // 2
    sibling = b + 1 - 2 * core
    column = chip // COL
    y = lax.rem(chip, COL)

    def chip_at(s):
        return lax.rem(column + s // COL, 2) * COL + lax.rem(y + lax.rem(s, COL), COL)

    def device_at(s):
        return 2 * chip_at(s) + core

    def remote(src, dst, send, recv, blk, dom):
        return pltpu.make_async_remote_copy(
            src_ref=src,
            dst_ref=dst,
            send_sem=send,
            recv_sem=recv,
            device_id=(blk, dom),
            device_id_type=MESH,
        )

    def await_bytes(ref, sem):
        pltpu.make_async_copy(ref, ref, sem).wait()

    def loop(lo, hi, body):
        def step(i, carry):
            body(i)
            return carry

        lax.fori_loop(lo, hi, step, 0)

    def block(i, n):
        return pl.ds(pl.multiple_of(i * n, n), n)

    loads = [
        pltpu.make_async_copy(src, dst, load_sem.at[i])
        for i, (src, dst) in enumerate(
            (
                (send_hbm, send_rows),
                (owner_hbm, owner_rows),
                (hw_hbm, hw_rows),
                (live_hbm, live_row),
                (feats_hbm, feats),
                (cot_hbm, cot),
                (tiles_hbm, tiles.at[:, pl.ds(1, TPG)]),
                (weight_hbm, weight),
            )
        )
    ]
    for load in loads:
        load.start()

    barrier = pltpu.get_barrier_semaphore()

    def greet_dom(k):
        pl.semaphore_signal(
            barrier, inc=1, device_id=(b, lax.rem(d + k, ND)), device_id_type=MESH
        )

    def greet_blk(k):
        pl.semaphore_signal(
            barrier, inc=1, device_id=(lax.rem(b + k, NB), d), device_id_type=MESH
        )

    loop(1, ND, greet_dom)
    loop(1, NB, greet_blk)

    for load in loads[:5]:
        load.wait()
    hw = hw_rows[...]
    hw_high = hw.astype(bf16)
    hw_low = (hw - hw_high.astype(f32)).astype(bf16)
    send = send_rows[...]
    owner = owner_rows[...]
    as_bf16 = lambda x: x.astype(f32).astype(bf16)
    stack = [as_bf16(send // 16), as_bf16(send % 16)]
    stack += [as_bf16(owner // 16), as_bf16(owner % 16), hw_high, hw_low]
    lane = lax.broadcasted_iota(jnp.int32, (SLOTS, LIST), 1)
    line = lax.broadcasted_iota(jnp.int32, (SLOTS, LIST), 0)
    spread = jnp.where(lane % SLOTS == line, 1.0, 0.0).astype(bf16)
    mine = lane // SLOTS == line

    def flat(x):
        return jnp.sum(jnp.where(mine, dot(x, spread), 0.0), axis=0, keepdims=True)

    rows = [flat(x) for x in stack]
    counts = jnp.broadcast_to(as_bf16(live_row[...]), (8, ND))
    count_row = dot(counts, jnp.where(mine, 1.0, 0.0).astype(bf16))[:1]
    slot = (lax.broadcasted_iota(jnp.int32, (1, LIST), 1) % SLOTS).astype(f32)
    send_row = jnp.where(slot < count_row, rows[0] * 16.0 + rows[1], -1.0)
    owner_row = rows[2] * 16.0 + rows[3]

    for i in range(PER):
        at = pl.ds(i * TILE, TILE)
        row = (lax.broadcasted_iota(jnp.int32, (TILE, LIST), 0) + i * TILE).astype(f32)
        pick[at, :] = jnp.where(row == send_row, 1.0, 0.0).astype(bf16)
    outgoing[...] = dot(pick[...], feats[...], 0, 0).astype(bf16)

    pl.semaphore_wait(barrier, ND + NB - 2)

    first, second = pl.ds(0, HALF), pl.ds(HALF, HALF)

    def lead_copy(s, half):
        at = gathered.at[b, half]
        return remote(
            feats.at[half], at, ag_send, ag_recv.at[s], device_at(s), d
        )

    def rest_copy(s, half):
        at = gathered.at[b, half]
        return remote(
            feats.at[half], at, ag_send, rest_recv.at[s], device_at(s), d
        )

    def back_at(s):
        return lax.rem(column + s // COL, 2) * COL + lax.rem(y + COL - lax.rem(s, COL), COL)

    def sib_copy(s):
        at = gathered.at[2 * back_at(s) + core]
        return remote(at, at, sib_send, sib_recv.at[s], sibling, d)

    def diag_y(j):
        at = gathered.at[device_at(COL), first]
        return remote(at, at, diag_send, diag_recv.at[j], device_at(j), d)

    def diag_x(j):
        at = gathered.at[2 * back_at(j) + core, second]
        return remote(at, at, diag_send, diag_recv.at[COL + j], device_at(COL), d)

    lead_copy(COL, first).start()
    for j in (1, 3, 2):
        lead_copy(j, second).start()
    rest_copy(COL, second).start()
    for j in (1, 3, 2):
        rest_copy(j, first).start()
    remote(feats, gathered.at[b], sib_send, sib_recv.at[0], sibling, d).start()

    def back_copy(k):
        q = lax.rem(d + k, ND)
        remote(
            back.at[block(q, SLOTS)],
            returned.at[block(d, SLOTS)],
            back_send,
            back_recv,
            b,
            q,
        ).start()

    def odd(i):
        back_copy(i + 1 + lax.rem(i, 2) * (ND - 1 - 2 * i))

    def even(i):
        back_copy(i + 2 + lax.rem(i, 2) * (ND - 3 - 2 * i))

    def dom_send(src, dst, send, recv):
        def body(i):
            half = i // 2
            k = half + 1 + lax.rem(i, 2) * (ND - 2 - 2 * half)
            q = lax.rem(d + k, ND)
            remote(
                src.at[block(q, SLOTS)], dst.at[block(d, SLOTS)], send, recv, b, q
            ).start()

        loop(0, ND - 1, body)

    dom_send(outgoing, incoming, out_send, out_recv)

    loads[5].wait()
    for i in range(PER):
        at = pl.ds(i * TILE, TILE)
        row = (lax.broadcasted_iota(jnp.int32, (TILE, LIST), 0) + i * TILE).astype(f32)
        hit = row == owner_row
        high[at, :] = jnp.where(hit, rows[4], 0.0).astype(bf16)
        low[at, :] = jnp.where(hit, rows[5], 0.0).astype(bf16)
    back[...] = (
        dot(high[...], cot[...], 0, 0) + dot(low[...], cot[...], 0, 0)
    ).astype(bf16)
    loop(0, ND // 2, odd)
    loop(0, 8, even)

    lead_copy(COL, first).wait_recv()
    for j in (1, 3, 2):
        diag_y(j).start()
    for j in (1, 3, 2):
        lead_copy(j, second).wait_recv()
        diag_x(j).start()

    zero = jnp.zeros((TILE, TILE), bf16)

    def clear(c):
        tiles[c, 0] = zero

    loop(0, NB, clear)
    loads[6].wait()

    def share(c):
        live = count_ref[c]
        spots = [jnp.where(t < live, pos_ref[t, 0, c], -1) for t in range(TPG)]
        for p in range(PER * PER):
            found = 0
            for t in range(TPG):
                found = jnp.where(spots[t] == p, t + 1, found)
            r, k = p // PER, p % PER
            adj[c, pl.ds(r * TILE, TILE), pl.ds(k * TILE, TILE)] = tiles[c, found]
        return dot(adj[c], cot[...], 0, 0).astype(bf16)

    def pair_copy(s):
        return remote(
            other.at[s], pair_got.at[s], pair_send, pair_recv.at[s], sibling, d
        )

    def other_step(i):
        s = lax.rem(i + COL + 1, CHIPS)
        other[s] = share(2 * chip_at(s) + 1 - core)
        pair_copy(s).start()

    loop(0, CHIPS, other_step)

    def whole_step(s):
        rest_copy(s, first).wait_recv()
        sib_copy(s).start()

    loop(1, COL + 1, whole_step)

    def own_step(i):
        s = lax.rem(i + COL + 1, CHIPS)
        own[s] = share(device_at(s))

    loop(0, CHIPS, own_step)

    def rs_first(j):
        return remote(
            pair_sum.at[COL + j, first], rs_y.at[j], rs_send, rs_recv.at[j], device_at(j), d
        )

    def rs_second(j):
        return remote(
            pair_sum.at[COL + j, second],
            rs_x.at[j],
            rs_send,
            rs_recv.at[COL + j],
            device_at(COL),
            d,
        )

    def sum_copy(s):
        return remote(
            pair_sum.at[s], rs_got.at[s], sum_send, sum_recv.at[s], device_at(s), d
        )

    def pair_step(s):
        pair_copy(s).wait_recv()
        pair_sum[s] = (own[s].astype(f32) + pair_got[s].astype(f32)).astype(bf16)

    def diag_step(j):
        pair_step(COL + j)
        rs_first(j).start()
        rs_second(j).start()

    loop(1, COL, diag_step)
    loop(1, COL + 1, pair_step)

    acc[...] = dot(adj[b], feats[...])

    def gain(at):
        acc[...] += dot(adj[at], gathered[at])

    loop(1, COL + 1, lambda s: gain(2 * back_at(s) + core))
    sib_copy(0).wait_recv()
    gain(sibling)

    def diag_wait(j):
        diag_y(j).wait_recv()
        diag_x(j).wait_recv()
        sib_copy(COL + j).start()
        gain(2 * back_at(COL + j) + core)

    loop(1, COL, diag_wait)

    def sib_step(s):
        sib_copy(s).wait_recv()
        gain(2 * back_at(s) + 1 - core)

    loop(1, CHIPS, sib_step)

    none = jnp.zeros((SLOTS, F), bf16)
    incoming[block(d, SLOTS), :] = none
    returned[block(d, SLOTS), :] = none
    others = pl.ds(0, LIST - SLOTS)
    await_bytes(incoming.at[others], out_recv)
    came = incoming[...]
    gained = (acc[...] + dot(high[...], came) + dot(low[...], came)).astype(bf16)
    whole = dot(gained, cot[...], 0, 0)
    side = lax.rem(d, 2)
    for i in range(2):
        half = whole[:, i * TILE : (i + 1) * TILE].reshape(NB, PIECE, TILE)
        term[i * NB : (i + 1) * NB] = half
        term16[i * NB : (i + 1) * NB] = half.astype(bf16)

    def plane_send(src_of, dst_of, stage):
        def body(n):
            flip = n // NB
            to = lax.rem(b + n, NB)
            to_side = lax.rem(side + flip, 2)
            remote(
                src_of(to_side * NB + to),
                dst_of(n),
                ar_send.at[stage],
                ar_recv.at[stage],
                to,
                d - side + to_side,
            ).start()

        loop(1, PLANE, body)

    place = side * NB + b
    plane_send(lambda n: term16.at[n], lambda n: got_a.at[n], 0)
    loads[7].wait()
    layer_ref[...] = dot(gained, weight[...]).astype(bf16)

    await_bytes(got_a.at[pl.ds(1, PLANE - 1)], ar_recv.at[0])
    piece = term[place]
    for n in range(1, PLANE):
        piece = piece + got_a[n].astype(f32)

    z = d // 2
    got_z[z] = piece.astype(bf16)

    def ring_send(k):
        at = got_z.at[z]
        to = lax.rem(d + 2 * k, ND)
        remote(at, at, ar_send.at[1], ar_recv.at[1], b, to).start()

    loop(1, RING, ring_send)
    loop(8, ND // 2 - 1, even)

    def column_sum(j):
        rs_second(j).wait_recv()
        at = pair_sum[j, HALF:].astype(f32) + rs_x[j].astype(f32)
        pair_sum[j, HALF:] = at.astype(bf16)
        sum_copy(j).start()

    def partner_sum(j):
        rs_first(j).wait_recv()

    loop(1, COL, partner_sum)
    both = pair_sum[COL, :HALF].astype(f32)
    for j in range(1, COL):
        both = both + rs_y[j].astype(f32)
    pair_sum[COL, :HALF] = both.astype(bf16)
    sum_copy(COL).start()
    loop(1, COL, column_sum)

    pair_copy(0).wait_recv()
    acc[...] = own[0].astype(f32) + pair_got[0].astype(f32)
    await_bytes(got_z.at[pl.ds(1, RING - 1)], ar_recv.at[1])
    piece = got_z[0].astype(f32)
    for k in range(1, RING):
        piece = piece + got_z[k].astype(f32)
    piece = (piece * (float(NB * ND * ROWS) ** -0.5)).astype(bf16)
    chunk[...] = piece
    plane_send(lambda n: chunk, lambda n: total.at[place], 2)
    total[place] = piece
    await_bytes(returned.at[others], back_recv)
    acc[...] += dot(pick[...], returned[...])

    def sum_step(s):
        sum_copy(s).wait_recv()
        acc[...] += rs_got[s].astype(f32)

    loop(1, COL + 1, sum_step)
    fgrad_ref[...] = dot(acc[...].astype(bf16), weight[...], 1, 1).astype(bf16)
    await_bytes(total.at[pl.ds(0, PLANE - 1)], ar_recv.at[2])
    for i in range(2):
        half = total[i * NB : (i + 1) * NB].astype(f32).reshape(F, TILE)
        wgrad_ref[:, i * TILE : (i + 1) * TILE] = half

    await_bytes(pair_got, pair_send)
    await_bytes(pair_sum.at[pl.ds(0, COL - 1)], rs_send)
    await_bytes(pair_sum.at[pl.ds(0, COL)], sum_send)
    await_bytes(returned.at[others], back_send)
    await_bytes(incoming.at[others], out_send)
    await_bytes(pair_sum.at[pl.ds(0, COL)], ag_send)
    await_bytes(pair_sum.at[pl.ds(0, COL - 1)], diag_send)
    await_bytes(pair_sum, sib_send)
    await_bytes(got_a.at[pl.ds(1, PLANE - 1)], ar_send.at[0])
    await_bytes(got_z.at[pl.ds(1, RING - 1)], ar_send.at[1])
    await_bytes(got_a.at[pl.ds(1, PLANE - 1)], ar_send.at[2])


def mesh_part(pos, count, tiles, feats, cot, weight, send, live, owner, hw):
    shape = jax.ShapeDtypeStruct
    far = pl.BlockSpec(memory_space=pltpu.HBM)
    near = pl.BlockSpec(memory_space=pltpu.VMEM)
    scalar = pl.BlockSpec(memory_space=pltpu.SMEM)
    dma = pltpu.SemaphoreType.DMA
    vmem = pltpu.VMEM
    return pl.pallas_call(
        mesh_kernel,
        out_shape=[
            shape((ROWS, F), bf16),
            shape((ROWS, F), bf16),
            shape((F, F), f32),
        ],
        in_specs=[scalar] * 2 + [far] * 8,
        out_specs=[near] * 3,
        scratch_shapes=[
            vmem((NB, TPG + 1, TILE, TILE), bf16),
            vmem((ROWS, F), bf16),
            vmem((ROWS, F), bf16),
            vmem((F, F), bf16),
            vmem((ND, SLOTS), jnp.int32),
            vmem((ND, SLOTS), jnp.int32),
            vmem((ND, SLOTS), f32),
            vmem((1, ND), jnp.int32),
            vmem((NB, ROWS, ROWS), bf16),
            vmem((ROWS, LIST), bf16),
            vmem((ROWS, LIST), bf16),
            vmem((ROWS, LIST), bf16),
            vmem((LIST, F), bf16),
            vmem((LIST, F), bf16),
            vmem((LIST, F), bf16),
            vmem((LIST, F), bf16),
            vmem((CHIPS, ROWS, F), bf16),
            vmem((CHIPS, ROWS, F), bf16),
            vmem((CHIPS, ROWS, F), bf16),
            vmem((CHIPS, ROWS, F), bf16),
            vmem((COL, HALF, F), bf16),
            vmem((COL, HALF, F), bf16),
            vmem((COL + 1, ROWS, F), bf16),
            vmem((NB, ROWS, F), bf16),
            vmem((ROWS, F), f32),
            vmem((PLANE, PIECE, TILE), f32),
            vmem((PLANE, PIECE, TILE), bf16),
            vmem((PIECE, TILE), bf16),
            vmem((PLANE, PIECE, TILE), bf16),
            vmem((RING, PIECE, TILE), bf16),
            vmem((PLANE, PIECE, TILE), bf16),
            dma((8,)),
            dma,
            dma((CHIPS,)),
            dma,
            dma((CHIPS,)),
            dma,
            dma((COL + 1,)),
            dma,
            dma,
            dma,
            dma,
            dma,
            dma((COL + 1,)),
            dma((COL + 1,)),
            dma,
            dma((CHIPS,)),
            dma,
            dma((CHIPS,)),
            dma((3,)),
            dma((3,)),
        ],
        compiler_params=pltpu.CompilerParams(
            collective_id=0, has_side_effects=True, vmem_limit_bytes=60 * MIB
        ),
    )(pos, count, tiles, feats, cot, weight, send, live, owner, hw)


def final_kernel(*refs):
    sources, targets, held, (load_sem, store_sem) = (
        refs[:3],
        refs[3:6],
        refs[6:9],
        refs[9:],
    )
    loads = [
        pltpu.make_async_copy(src, at, load_sem.at[i])
        for i, (src, at) in enumerate(zip(sources, held))
    ]
    stores = [
        pltpu.make_async_copy(at, dst, store_sem.at[i])
        for i, (at, dst) in enumerate(zip(held, targets))
    ]
    for load in loads:
        load.start()
    for load, store in zip(loads, stores):
        load.wait()
        store.start()
    for store in stores:
        store.wait()


def final_part(*results):
    far = pl.BlockSpec(memory_space=pltpu.HBM)
    return pl.pallas_call(
        final_kernel,
        out_shape=[jax.ShapeDtypeStruct(x.shape, x.dtype) for x in results],
        in_specs=[far] * 3,
        out_specs=[far] * 3,
        scratch_shapes=[pltpu.VMEM(x.shape, x.dtype) for x in results]
        + [pltpu.SemaphoreType.DMA((3,))] * 2,
        compiler_params=pltpu.CompilerParams(vmem_limit_bytes=60 * MIB),
    )(*results)


def on_device(
    features,
    weight,
    tiles,
    tile_pos,
    tile_count,
    send_list,
    send_count,
    owner_map,
    halo_weight,
    cotangent,
):
    results = mesh_part(
        jnp.transpose(tile_pos, (0, 3, 1, 2))[0],
        tile_count[0, 0],
        tiles[0, 0],
        features[0],
        cotangent[0],
        weight,
        send_list[0, 0],
        send_count[0],
        owner_map[0, 0],
        halo_weight[0, 0],
    )
    layer_out, feature_grad, weight_grad = final_part(*results)
    return (layer_out[None], feature_grad[None], weight_grad)


def solution(mesh):
    return jax.shard_map(
        on_device,
        mesh=mesh,
        in_specs=(
            P("dom", "blk", None),
            P(),
            P("dom", "blk", None, None, None, None),
            P("dom", "blk", None, None),
            P("dom", "blk", None),
            P("dom", "blk", None, None),
            P("dom", "blk", None),
            P("dom", "blk", None, None),
            P("dom", "blk", None, None),
            P("dom", "blk", None),
        ),
        out_specs=(P("dom", "blk", None), P("dom", "blk", None), P()),
        check_vma=False,
    )
```

```python
import functools

import jax
import jax.numpy as jnp
from jax import lax
from jax.experimental import pallas as pl
from jax.experimental.pallas import tpu as pltpu
from jax.sharding import PartitionSpec as P

MESH = pl.DeviceIdType.MESH
NB = 16
ND = 32
CHIPS = NB // 2
COL = 4
HALF = 256
TILE = 128
PER = 4
ROWS = TILE * PER
TPG = 6
F = 256
SLOTS = 32
LIST = ND * SLOTS
PIECE = F // NB
PLANE = 2 * NB
RING = ND // 2
MIB = 1 << 20

bf16 = jnp.bfloat16
f32 = jnp.float32


def dot(a, b, ca=1, cb=0):
    return lax.dot_general(a, b, (((ca,), (cb,)), ((), ())), preferred_element_type=f32)


def mesh_kernel(
    pos_ref,
    count_ref,
    tiles_hbm,
    feats_hbm,
    cot_hbm,
    weight_hbm,
    send_hbm,
    live_hbm,
    owner_hbm,
    hw_hbm,
    layer_ref,
    fgrad_ref,
    wgrad_ref,
    tiles,
    feats,
    cot,
    weight,
    send_rows,
    owner_rows,
    hw_rows,
    live_row,
    adj,
    pick,
    high,
    low,
    outgoing,
    back,
    returned,
    incoming,
    other,
    own,
    pair_got,
    pair_sum,
    rs_y,
    rs_x,
    rs_got,
    gathered,
    acc,
    term,
    term16,
    chunk,
    got_a,
    got_z,
    total,
    load_sem,
    pair_send,
    pair_recv,
    rs_send,
    rs_recv,
    sum_send,
    sum_recv,
    back_send,
    back_recv,
    out_send,
    out_recv,
    ag_send,
    ag_recv,
    rest_recv,
    diag_send,
    diag_recv,
    sib_send,
    sib_recv,
    ar_send,
    ar_recv,
):
    b = lax.axis_index("blk")
    d = lax.axis_index("dom")
    core = lax.rem(b, 2)
    chip = b // 2
    sibling = b + 1 - 2 * core
    column = chip // COL
    y = lax.rem(chip, COL)

    def chip_at(s):
        return lax.rem(column + s // COL, 2) * COL + lax.rem(y + lax.rem(s, COL), COL)

    def device_at(s):
        return 2 * chip_at(s) + core

    def remote(src, dst, send, recv, blk, dom):
        return pltpu.make_async_remote_copy(
            src_ref=src,
            dst_ref=dst,
            send_sem=send,
            recv_sem=recv,
            device_id=(blk, dom),
            device_id_type=MESH,
        )

    def await_bytes(ref, sem):
        pltpu.make_async_copy(ref, ref, sem).wait()

    def loop(lo, hi, body):
        def step(i, carry):
            body(i)
            return carry

        lax.fori_loop(lo, hi, step, 0)

    def block(i, n):
        return pl.ds(pl.multiple_of(i * n, n), n)

    loads = [
        pltpu.make_async_copy(src, dst, load_sem.at[i])
        for i, (src, dst) in enumerate(
            (
                (send_hbm, send_rows),
                (owner_hbm, owner_rows),
                (hw_hbm, hw_rows),
                (live_hbm, live_row),
                (feats_hbm, feats),
                (cot_hbm, cot),
                (tiles_hbm, tiles.at[:, pl.ds(1, TPG)]),
                (weight_hbm, weight),
            )
        )
    ]
    for load in loads:
        load.start()

    barrier = pltpu.get_barrier_semaphore()

    def greet_dom(k):
        pl.semaphore_signal(
            barrier, inc=1, device_id=(b, lax.rem(d + k, ND)), device_id_type=MESH
        )

    def greet_blk(k):
        pl.semaphore_signal(
            barrier, inc=1, device_id=(lax.rem(b + k, NB), d), device_id_type=MESH
        )

    loop(1, ND, greet_dom)
    loop(1, NB, greet_blk)

    for load in loads[:5]:
        load.wait()
    hw = hw_rows[...]
    hw_high = hw.astype(bf16)
    hw_low = (hw - hw_high.astype(f32)).astype(bf16)
    send = send_rows[...]
    owner = owner_rows[...]
    as_bf16 = lambda x: x.astype(f32).astype(bf16)
    stack = [as_bf16(send // 16), as_bf16(send % 16)]
    stack += [as_bf16(owner // 16), as_bf16(owner % 16), hw_high, hw_low]
    lane = lax.broadcasted_iota(jnp.int32, (SLOTS, LIST), 1)
    line = lax.broadcasted_iota(jnp.int32, (SLOTS, LIST), 0)
    spread = jnp.where(lane % SLOTS == line, 1.0, 0.0).astype(bf16)
    mine = lane // SLOTS == line

    def flat(x):
        return jnp.sum(jnp.where(mine, dot(x, spread), 0.0), axis=0, keepdims=True)

    rows = [flat(x) for x in stack]
    counts = jnp.broadcast_to(as_bf16(live_row[...]), (8, ND))
    count_row = dot(counts, jnp.where(mine, 1.0, 0.0).astype(bf16))[:1]
    slot = (lax.broadcasted_iota(jnp.int32, (1, LIST), 1) % SLOTS).astype(f32)
    send_row = jnp.where(slot < count_row, rows[0] * 16.0 + rows[1], -1.0)
    owner_row = rows[2] * 16.0 + rows[3]

    for i in range(PER):
        at = pl.ds(i * TILE, TILE)
        row = (lax.broadcasted_iota(jnp.int32, (TILE, LIST), 0) + i * TILE).astype(f32)
        pick[at, :] = jnp.where(row == send_row, 1.0, 0.0).astype(bf16)
    outgoing[...] = dot(pick[...], feats[...], 0, 0).astype(bf16)

    pl.semaphore_wait(barrier, ND + NB - 2)

    first, second = pl.ds(0, HALF), pl.ds(HALF, HALF)

    def lead_copy(s, half):
        at = gathered.at[b, half]
        return remote(
            feats.at[half], at, ag_send, ag_recv.at[s], device_at(s), d
        )

    def rest_copy(s, half):
        at = gathered.at[b, half]
        return remote(
            feats.at[half], at, ag_send, rest_recv.at[s], device_at(s), d
        )

    def back_at(s):
        return lax.rem(column + s // COL, 2) * COL + lax.rem(y + COL - lax.rem(s, COL), COL)

    def sib_copy(s):
        at = gathered.at[2 * back_at(s) + core]
        return remote(at, at, sib_send, sib_recv.at[s], sibling, d)

    def diag_y(j):
        at = gathered.at[device_at(COL), first]
        return remote(at, at, diag_send, diag_recv.at[j], device_at(j), d)

    def diag_x(j):
        at = gathered.at[2 * back_at(j) + core, second]
        return remote(at, at, diag_send, diag_recv.at[COL + j], device_at(COL), d)

    lead_copy(COL, first).start()
    for j in (1, 3, 2):
        lead_copy(j, second).start()
    rest_copy(COL, second).start()
    for j in (1, 3, 2):
        rest_copy(j, first).start()
    remote(feats, gathered.at[b], sib_send, sib_recv.at[0], sibling, d).start()

    def back_copy(k):
        q = lax.rem(d + k, ND)
        remote(
            back.at[block(q, SLOTS)],
            returned.at[block(d, SLOTS)],
            back_send,
            back_recv,
            b,
            q,
        ).start()

    def odd(i):
        back_copy(i + 1 + lax.rem(i, 2) * (ND - 1 - 2 * i))

    def even(i):
        back_copy(i + 2 + lax.rem(i, 2) * (ND - 3 - 2 * i))

    def dom_send(src, dst, send, recv):
        def body(i):
            half = i // 2
            k = half + 1 + lax.rem(i, 2) * (ND - 2 - 2 * half)
            q = lax.rem(d + k, ND)
            remote(
                src.at[block(q, SLOTS)], dst.at[block(d, SLOTS)], send, recv, b, q
            ).start()

        loop(0, ND - 1, body)

    dom_send(outgoing, incoming, out_send, out_recv)

    loads[5].wait()
    for i in range(PER):
        at = pl.ds(i * TILE, TILE)
        row = (lax.broadcasted_iota(jnp.int32, (TILE, LIST), 0) + i * TILE).astype(f32)
        hit = row == owner_row
        high[at, :] = jnp.where(hit, rows[4], 0.0).astype(bf16)
        low[at, :] = jnp.where(hit, rows[5], 0.0).astype(bf16)
    back[...] = (
        dot(high[...], cot[...], 0, 0) + dot(low[...], cot[...], 0, 0)
    ).astype(bf16)
    loop(0, ND // 2, odd)
    loop(0, 8, even)

    lead_copy(COL, first).wait_recv()
    for j in (1, 3, 2):
        diag_y(j).start()
    for j in (1, 3, 2):
        lead_copy(j, second).wait_recv()
        diag_x(j).start()

    zero = jnp.zeros((TILE, TILE), bf16)

    def clear(c):
        tiles[c, 0] = zero

    loop(0, NB, clear)
    loads[6].wait()

    def build(c):
        live = count_ref[c]
        spots = [jnp.where(t < live, pos_ref[t, 0, c], -1) for t in range(TPG)]
        for p in range(PER * PER):
            found = 0
            for t in range(TPG):
                found = jnp.where(spots[t] == p, t + 1, found)
            r, k = p // PER, p % PER
            adj[c, pl.ds(r * TILE, TILE), pl.ds(k * TILE, TILE)] = tiles[c, found]

    def share(c):
        return dot(adj[c], cot[...], 0, 0).astype(bf16)

    def pair_copy(s):
        return remote(
            other.at[s], pair_got.at[s], pair_send, pair_recv.at[s], sibling, d
        )

    def other_step(i):
        s = lax.rem(i + COL + 1, CHIPS)
        c = 2 * chip_at(s) + 1 - core
        build(c)
        other[s] = share(c)
        pair_copy(s).start()

    loop(0, CHIPS, other_step)

    def whole_step(s):
        rest_copy(s, first).wait_recv()
        sib_copy(s).start()

    loop(1, COL + 1, whole_step)

    def own_step(i):
        s = lax.rem(i + COL + 1, CHIPS)
        own[s] = share(device_at(s))

    loop(0, NB // 2, lambda i: build(2 * i + core))

    def rs_first(j):
        return remote(
            pair_sum.at[COL + j, first], rs_y.at[j], rs_send, rs_recv.at[j], device_at(j), d
        )

    def rs_second(j):
        return remote(
            pair_sum.at[COL + j, second],
            rs_x.at[j],
            rs_send,
            rs_recv.at[COL + j],
            device_at(COL),
            d,
        )

    def sum_copy(s):
        return remote(
            pair_sum.at[s], rs_got.at[s], sum_send, sum_recv.at[s], device_at(s), d
        )

    def pair_step(s):
        pair_copy(s).wait_recv()
        pair_sum[s] = (own[s].astype(f32) + pair_got[s].astype(f32)).astype(bf16)

    def diag_step(j):
        pair_step(COL + j)
        rs_first(j).start()
        rs_second(j).start()


    acc[...] = dot(adj[b], feats[...])

    def gain(at):
        acc[...] += dot(adj[at], gathered[at])

    loop(1, COL + 1, lambda s: gain(2 * back_at(s) + core))
    sib_copy(0).wait_recv()
    gain(sibling)

    def diag_wait(j):
        diag_y(j).wait_recv()
        diag_x(j).wait_recv()
        sib_copy(COL + j).start()
        gain(2 * back_at(COL + j) + core)

    loop(1, COL, diag_wait)

    def sib_step(s):
        sib_copy(s).wait_recv()
        gain(2 * back_at(s) + 1 - core)

    loop(1, CHIPS, sib_step)

    none = jnp.zeros((SLOTS, F), bf16)
    incoming[block(d, SLOTS), :] = none
    returned[block(d, SLOTS), :] = none
    others = pl.ds(0, LIST - SLOTS)
    await_bytes(incoming.at[others], out_recv)
    came = incoming[...]
    gained = (acc[...] + dot(high[...], came) + dot(low[...], came)).astype(bf16)
    whole = dot(gained, cot[...], 0, 0)
    side = lax.rem(d, 2)
    for i in range(2):
        half = whole[:, i * TILE : (i + 1) * TILE].reshape(NB, PIECE, TILE)
        term[i * NB : (i + 1) * NB] = half
        term16[i * NB : (i + 1) * NB] = half.astype(bf16)

    def plane_send(src_of, dst_of, stage):
        def body(n):
            flip = n // NB
            to = lax.rem(b + n, NB)
            to_side = lax.rem(side + flip, 2)
            remote(
                src_of(to_side * NB + to),
                dst_of(n),
                ar_send.at[stage],
                ar_recv.at[stage],
                to,
                d - side + to_side,
            ).start()

        loop(1, PLANE, body)

    place = side * NB + b
    plane_send(lambda n: term16.at[n], lambda n: got_a.at[n], 0)
    loads[7].wait()
    layer_ref[...] = dot(gained, weight[...]).astype(bf16)

    loop(0, CHIPS, own_step)
    loop(1, COL, diag_step)
    loop(1, COL + 1, pair_step)
    await_bytes(got_a.at[pl.ds(1, PLANE - 1)], ar_recv.at[0])
    piece = term[place]
    for n in range(1, PLANE):
        piece = piece + got_a[n].astype(f32)

    z = d // 2
    got_z[z] = piece.astype(bf16)

    def ring_send(k):
        at = got_z.at[z]
        to = lax.rem(d + 2 * k, ND)
        remote(at, at, ar_send.at[1], ar_recv.at[1], b, to).start()

    loop(1, RING, ring_send)
    loop(8, ND // 2 - 1, even)

    def column_sum(j):
        rs_second(j).wait_recv()
        at = pair_sum[j, HALF:].astype(f32) + rs_x[j].astype(f32)
        pair_sum[j, HALF:] = at.astype(bf16)
        sum_copy(j).start()

    def partner_sum(j):
        rs_first(j).wait_recv()

    loop(1, COL, partner_sum)
    both = pair_sum[COL, :HALF].astype(f32)
    for j in range(1, COL):
        both = both + rs_y[j].astype(f32)
    pair_sum[COL, :HALF] = both.astype(bf16)
    sum_copy(COL).start()
    loop(1, COL, column_sum)

    pair_copy(0).wait_recv()
    acc[...] = own[0].astype(f32) + pair_got[0].astype(f32)
    await_bytes(got_z.at[pl.ds(1, RING - 1)], ar_recv.at[1])
    piece = got_z[0].astype(f32)
    for k in range(1, RING):
        piece = piece + got_z[k].astype(f32)
    piece = (piece * (float(NB * ND * ROWS) ** -0.5)).astype(bf16)
    chunk[...] = piece
    plane_send(lambda n: chunk, lambda n: total.at[place], 2)
    total[place] = piece
    await_bytes(returned.at[others], back_recv)
    acc[...] += dot(pick[...], returned[...])

    def sum_step(s):
        sum_copy(s).wait_recv()
        acc[...] += rs_got[s].astype(f32)

    loop(1, COL + 1, sum_step)
    fgrad_ref[...] = dot(acc[...].astype(bf16), weight[...], 1, 1).astype(bf16)
    await_bytes(total.at[pl.ds(0, PLANE - 1)], ar_recv.at[2])
    for i in range(2):
        half = total[i * NB : (i + 1) * NB].astype(f32).reshape(F, TILE)
        wgrad_ref[:, i * TILE : (i + 1) * TILE] = half

    await_bytes(pair_got, pair_send)
    await_bytes(pair_sum.at[pl.ds(0, COL - 1)], rs_send)
    await_bytes(pair_sum.at[pl.ds(0, COL)], sum_send)
    await_bytes(returned.at[others], back_send)
    await_bytes(incoming.at[others], out_send)
    await_bytes(pair_sum.at[pl.ds(0, COL)], ag_send)
    await_bytes(pair_sum.at[pl.ds(0, COL - 1)], diag_send)
    await_bytes(pair_sum, sib_send)
    await_bytes(got_a.at[pl.ds(1, PLANE - 1)], ar_send.at[0])
    await_bytes(got_z.at[pl.ds(1, RING - 1)], ar_send.at[1])
    await_bytes(got_a.at[pl.ds(1, PLANE - 1)], ar_send.at[2])


def mesh_part(pos, count, tiles, feats, cot, weight, send, live, owner, hw):
    shape = jax.ShapeDtypeStruct
    far = pl.BlockSpec(memory_space=pltpu.HBM)
    near = pl.BlockSpec(memory_space=pltpu.VMEM)
    scalar = pl.BlockSpec(memory_space=pltpu.SMEM)
    dma = pltpu.SemaphoreType.DMA
    vmem = pltpu.VMEM
    return pl.pallas_call(
        mesh_kernel,
        out_shape=[
            shape((ROWS, F), bf16),
            shape((ROWS, F), bf16),
            shape((F, F), f32),
        ],
        in_specs=[scalar] * 2 + [far] * 8,
        out_specs=[near] * 3,
        scratch_shapes=[
            vmem((NB, TPG + 1, TILE, TILE), bf16),
            vmem((ROWS, F), bf16),
            vmem((ROWS, F), bf16),
            vmem((F, F), bf16),
            vmem((ND, SLOTS), jnp.int32),
            vmem((ND, SLOTS), jnp.int32),
            vmem((ND, SLOTS), f32),
            vmem((1, ND), jnp.int32),
            vmem((NB, ROWS, ROWS), bf16),
            vmem((ROWS, LIST), bf16),
            vmem((ROWS, LIST), bf16),
            vmem((ROWS, LIST), bf16),
            vmem((LIST, F), bf16),
            vmem((LIST, F), bf16),
            vmem((LIST, F), bf16),
            vmem((LIST, F), bf16),
            vmem((CHIPS, ROWS, F), bf16),
            vmem((CHIPS, ROWS, F), bf16),
            vmem((CHIPS, ROWS, F), bf16),
            vmem((CHIPS, ROWS, F), bf16),
            vmem((COL, HALF, F), bf16),
            vmem((COL, HALF, F), bf16),
            vmem((COL + 1, ROWS, F), bf16),
            vmem((NB, ROWS, F), bf16),
            vmem((ROWS, F), f32),
            vmem((PLANE, PIECE, TILE), f32),
            vmem((PLANE, PIECE, TILE), bf16),
            vmem((PIECE, TILE), bf16),
            vmem((PLANE, PIECE, TILE), bf16),
            vmem((RING, PIECE, TILE), bf16),
            vmem((PLANE, PIECE, TILE), bf16),
            dma((8,)),
            dma,
            dma((CHIPS,)),
            dma,
            dma((CHIPS,)),
            dma,
            dma((COL + 1,)),
            dma,
            dma,
            dma,
            dma,
            dma,
            dma((COL + 1,)),
            dma((COL + 1,)),
            dma,
            dma((CHIPS,)),
            dma,
            dma((CHIPS,)),
            dma((3,)),
            dma((3,)),
        ],
        compiler_params=pltpu.CompilerParams(
            collective_id=0, has_side_effects=True, vmem_limit_bytes=60 * MIB
        ),
    )(pos, count, tiles, feats, cot, weight, send, live, owner, hw)


def final_kernel(*refs):
    sources, targets, held, (load_sem, store_sem) = (
        refs[:3],
        refs[3:6],
        refs[6:9],
        refs[9:],
    )
    loads = [
        pltpu.make_async_copy(src, at, load_sem.at[i])
        for i, (src, at) in enumerate(zip(sources, held))
    ]
    stores = [
        pltpu.make_async_copy(at, dst, store_sem.at[i])
        for i, (at, dst) in enumerate(zip(held, targets))
    ]
    for load in loads:
        load.start()
    for load, store in zip(loads, stores):
        load.wait()
        store.start()
    for store in stores:
        store.wait()


def final_part(*results):
    far = pl.BlockSpec(memory_space=pltpu.HBM)
    return pl.pallas_call(
        final_kernel,
        out_shape=[jax.ShapeDtypeStruct(x.shape, x.dtype) for x in results],
        in_specs=[far] * 3,
        out_specs=[far] * 3,
        scratch_shapes=[pltpu.VMEM(x.shape, x.dtype) for x in results]
        + [pltpu.SemaphoreType.DMA((3,))] * 2,
        compiler_params=pltpu.CompilerParams(vmem_limit_bytes=60 * MIB),
    )(*results)


def on_device(
    features,
    weight,
    tiles,
    tile_pos,
    tile_count,
    send_list,
    send_count,
    owner_map,
    halo_weight,
    cotangent,
):
    results = mesh_part(
        jnp.transpose(tile_pos, (0, 3, 1, 2))[0],
        tile_count[0, 0],
        tiles[0, 0],
        features[0],
        cotangent[0],
        weight,
        send_list[0, 0],
        send_count[0],
        owner_map[0, 0],
        halo_weight[0, 0],
    )
    layer_out, feature_grad, weight_grad = final_part(*results)
    return (layer_out[None], feature_grad[None], weight_grad)


def solution(mesh):
    return jax.shard_map(
        on_device,
        mesh=mesh,
        in_specs=(
            P("dom", "blk", None),
            P(),
            P("dom", "blk", None, None, None, None),
            P("dom", "blk", None, None),
            P("dom", "blk", None),
            P("dom", "blk", None, None),
            P("dom", "blk", None),
            P("dom", "blk", None, None),
            P("dom", "blk", None, None),
            P("dom", "blk", None),
        ),
        out_specs=(P("dom", "blk", None), P("dom", "blk", None), P()),
        check_vma=False,
    )
```
